512 devices in a mesh: grp: 16 (over y, core), ta: 4 (over z_hi), ha: 8 (over x, z_lo).
Axes of the slice: x: 4, y: 8, z: 8 (z_hi: 4, z_lo: 2; z = z_hi * 2 + z_lo), core: 2. Of those that a mesh axis runs over, the one named last changes fastest.
Arguments:
- queries: bfloat16 [64, 8, 128, 1536], P(('grp', 'ta'), 'ha'), parts along dimension 0, may hold values from -6 to 6
- key_tiles: bfloat16 [64, 8, 128, 1536], P(('grp', 'ta'), 'ha'), parts along dimension 0, may hold values from -6 to 6
- value_tiles: bfloat16 [64, 8, 128, 1536], P(('grp', 'ta'), 'ha'), parts along dimension 0, may hold values from -6 to 6
- outputs: bfloat16 [64, 8, 128, 1536], P(('grp', 'ta'), 'ha'), parts along dimension 0, may hold values from -6 to 6
- grads_out: bfloat16 [64, 8, 128, 1536], P(('grp', 'ta'), 'ha'), parts along dimension 0, may hold values from -6 to 6
- log_sums: float32 [64, 8, 12, 128], P(('grp', 'ta'), 'ha'), parts along dimension 0, may hold values from 4 to 7
- tile_counts: int32 [64, 8], P('grp'), parts along dimension 0, may hold values from 32 to 128, as said below
- head_reach: int32 [12, 2], replicated, may hold values from 0 to 1, as said below
Outputs:
- query_grads: bfloat16 [64, 8, 128, 1536], P(('grp', 'ta'), 'ha'), parts along dimension 0
- key_grads: bfloat16 [64, 8, 128, 1536], P(('grp', 'ta'), 'ha'), parts along dimension 0
- value_grads: bfloat16 [64, 8, 128, 1536], P(('grp', 'ta'), 'ha'), parts along dimension 0
The draws below stay inside these ranges and needn't reach their ends.
There are 16 independent parts, one for each index of `grp`. The reference program is written for one: setup_inputs(seed, part) draws one part's arguments, and reference() takes and returns one part's arrays. A program takes and returns all parts, laid end to end along the dimension named above; an argument that names none is the same for every part. Nothing has to cross between parts.
Inputs may be any that keep to these rules, and one draw needn't show every extreme that they name: `tile_counts`: tiles outside the last time row and the last height column hold all 128 tokens; the tile in the last row and last column holds 32. `head_reach`: some head reaches 1 along both axes and some head 0 along both.
All inputs are finite; a program needn't handle non-finite values.
Results may differ from the reference program's by a relative error of at most 0.0057.
Values may be sent and summed in bfloat16 or wider, within the bound.
A program may use at most 128 MiB of HBM per device.

```python
import jax
import jax.numpy as jnp
from jax import lax

HEADS = 12
HEAD_DIM = 128
TILE_TOK = 128
FEAT = 1536
TILES_T = 4
TILES_H = 8


def draw_tile_counts(key, part):
    key = jax.random.fold_in(key, 11)
    ragged = jax.random.randint(key, (TILES_T, TILES_H), TILE_TOK // 4, TILE_TOK + 1)
    row_ids = jnp.arange(TILES_T)[:, None]
    col_ids = jnp.arange(TILES_H)[None, :]
    on_edge = (row_ids == TILES_T - 1) | (col_ids == TILES_H - 1)
    counts_all = jnp.where(on_edge, ragged, TILE_TOK)
    counts_all = counts_all.at[TILES_T - 1, TILES_H - 1].set(TILE_TOK // 4)
    return counts_all.astype(jnp.int32)


def draw_head_reach(key, part):
    key = jax.random.fold_in(key, 23)
    bit_key, perm_key = jax.random.split(key)
    reach_bits = jax.random.randint(bit_key, (HEADS, 2), 0, 2)
    order = jax.random.permutation(perm_key, HEADS)
    reach_bits = reach_bits.at[order[0]].set(1)
    reach_bits = reach_bits.at[order[1]].set(0)
    return reach_bits.astype(jnp.int32)


def shard_levels(own_key, shape, pieces, smallest, largest):
    factor_of, own = 1.0, jax.random.fold_in(own_key, 6)
    for position, shards_of in pieces:
        draws = jnp.exp(jax.random.uniform(jax.random.fold_in(own, position), (shards_of,), jnp.float32, smallest / len(pieces), largest / len(pieces)))
        factor_of = factor_of * jnp.repeat(draws, shape[position] // shards_of).reshape([-1 if axis == position else 1 for axis in range(len(shape))])
    return factor_of


def normal_values(rng, dims, width, limit, pieces=(), kind=jnp.bfloat16):
    drawn = width * jax.random.normal(rng, dims, jnp.float32)
    if pieces:
        drawn = drawn * shard_levels(rng, dims, pieces, -0.22, 0.18)
    return jnp.clip(drawn, -limit, limit).astype(kind)


def setup_inputs(seed: int = 0, part: int = 0) -> dict:
    key_of = jax.random.split(jax.random.key(seed), 9)
    own_keys = jax.random.split(jax.random.fold_in(key_of[8], part), 9)
    queries = normal_values(own_keys[0], (TILES_T, TILES_H, TILE_TOK, FEAT), 1.0, 6.0, ((0, 4), (1, 8)))
    key_tiles = normal_values(own_keys[1], (TILES_T, TILES_H, TILE_TOK, FEAT), 1.0, 6.0, ((0, 4), (1, 8)))
    value_tiles = normal_values(own_keys[2], (TILES_T, TILES_H, TILE_TOK, FEAT), 1.0, 6.0, ((0, 4), (1, 8)))
    outputs = normal_values(own_keys[3], (TILES_T, TILES_H, TILE_TOK, FEAT), 1.0, 6.0, ((0, 4), (1, 8)))
    grads_out = normal_values(own_keys[4], (TILES_T, TILES_H, TILE_TOK, FEAT), 1.0, 6.0, ((0, 4), (1, 8)))
    log_sums = jnp.clip(4.0 + 3.0 * jax.random.uniform(own_keys[5], (TILES_T, TILES_H, HEADS, TILE_TOK), jnp.float32) ** shard_levels(own_keys[5], (TILES_T, TILES_H, HEADS, TILE_TOK), ((0, 4), (1, 8)), -0.2, 0.2), 4.0, 7.0)
    tile_counts = draw_tile_counts(jax.random.fold_in(jax.random.fold_in(key_of[8], part), 71), part)
    head_reach = draw_head_reach(jax.random.fold_in(key_of[8], 71), part)
    return {"queries": queries, "key_tiles": key_tiles, "value_tiles": value_tiles, "outputs": outputs, "grads_out": grads_out, "log_sums": log_sums, "tile_counts": tile_counts, "head_reach": head_reach}


def slot_allowed(head_reach):
    slot_ids = jnp.arange(9)
    step_t = jnp.abs(slot_ids // 3 - 1)
    step_h = jnp.abs(slot_ids % 3 - 1)
    return (step_t[None, :] <= head_reach[:, 0:1]) & (step_h[None, :] <= head_reach[:, 1:2])


def attend_back(query_rows, grad_rows, lse_rows, delta_rows, key_rows, value_rows, full_mask):
    score_scale = HEAD_DIM ** -0.5
    hp = lax.Precision.HIGHEST
    scores = jnp.einsum("rhd,chd->hrc", query_rows.astype(jnp.float32), key_rows.astype(jnp.float32), precision=hp) * score_scale
    soft_probs = jnp.where(full_mask, jnp.exp(scores - lse_rows[:, :, None]), jnp.float32(0.0))
    dprobs = jnp.einsum("rhd,chd->hrc", grad_rows.astype(jnp.float32), value_rows.astype(jnp.float32), precision=hp)
    score_grads = (soft_probs * (dprobs - delta_rows[:, :, None]) * score_scale).astype(jnp.bfloat16)
    return soft_probs.astype(jnp.bfloat16), score_grads


def reference(queries, key_tiles, value_tiles, outputs, grads_out, log_sums, tile_counts, head_reach):
    tok_rows = TILE_TOK
    hp = lax.Precision.HIGHEST
    pad_keys = jnp.pad(key_tiles, ((1, 1), (1, 1), (0, 0), (0, 0)))
    pad_values = jnp.pad(value_tiles, ((1, 1), (1, 1), (0, 0), (0, 0)))
    pad_counts = jnp.pad(tile_counts, 1)
    allowed = slot_allowed(head_reach)

    def one_tile(tile_index):
        place_t = (tile_index // TILES_H).astype(jnp.int32)
        place_h = (tile_index % TILES_H).astype(jnp.int32)
        zero = jnp.int32(0)
        near_counts = lax.dynamic_slice(pad_counts, (place_t, place_h), (3, 3)).reshape(9)
        near_live = jnp.arange(tok_rows)[None, :] < near_counts[:, None]
        own_live = jnp.arange(tok_rows) < near_counts[4]
        key_mask = (allowed[:, :, None] & near_live[None]).reshape(HEADS, 9 * tok_rows)
        full_mask = key_mask[:, None, :] & own_live[None, :, None]
        near_keys = lax.dynamic_slice(pad_keys, (place_t, place_h, zero, zero), (3, 3, tok_rows, FEAT)).reshape(9 * tok_rows, HEADS, HEAD_DIM)
        near_values = lax.dynamic_slice(pad_values, (place_t, place_h, zero, zero), (3, 3, tok_rows, FEAT)).reshape(9 * tok_rows, HEADS, HEAD_DIM)
        query_tile = queries[place_t, place_h].reshape(tok_rows, HEADS, HEAD_DIM)
        grad_tile = grads_out[place_t, place_h].reshape(tok_rows, HEADS, HEAD_DIM)
        out_tile = outputs[place_t, place_h].reshape(tok_rows, HEADS, HEAD_DIM)
        row_delta = jnp.sum(grad_tile.astype(jnp.float32) * out_tile.astype(jnp.float32), axis=2).T
        soft_probs, score_grads = attend_back(query_tile, grad_tile, log_sums[place_t, place_h], row_delta, near_keys, near_values, full_mask)
        dquery = jnp.einsum("hrc,chd->rhd", score_grads.astype(jnp.float32), near_keys.astype(jnp.float32), precision=hp).astype(jnp.bfloat16)
        dkey_part = jnp.einsum("hrc,rhd->chd", score_grads.astype(jnp.float32), query_tile.astype(jnp.float32), precision=hp).astype(jnp.bfloat16)
        dval_part = jnp.einsum("hrc,rhd->chd", soft_probs.astype(jnp.float32), grad_tile.astype(jnp.float32), precision=hp).astype(jnp.bfloat16)
        grad_parts = jnp.stack([dkey_part, dval_part]).reshape(2, 3, 3, tok_rows, FEAT)
        return dquery.reshape(tok_rows, FEAT), grad_parts

    dqueries, all_parts = lax.map(one_tile, jnp.arange(TILES_T * TILES_H, dtype=jnp.int32))
    query_grads = dqueries.reshape(TILES_T, TILES_H, tok_rows, FEAT)
    all_parts = all_parts.reshape(TILES_T, TILES_H, 2, 3, 3, tok_rows, FEAT)
    accum = jnp.zeros((2, TILES_T + 2, TILES_H + 2, tok_rows, FEAT), jnp.float32)
    for shift_t in range(3):
        for shift_h in range(3):
            piece = jnp.transpose(all_parts[:, :, :, shift_t, shift_h].astype(jnp.float32), (2, 0, 1, 3, 4))
            accum = accum.at[:, shift_t:shift_t + TILES_T, shift_h:shift_h + TILES_H].add(piece)
    grad_total = accum[:, 1:-1, 1:-1].astype(jnp.bfloat16)
    return query_grads, grad_total[0], grad_total[1]
```

```python
import functools
import math

import jax
import jax.numpy as jnp
from jax import lax
from jax.experimental import pallas as pl
from jax.experimental.pallas import tpu as pltpu
from jax.sharding import PartitionSpec as P

HEADS = 12
HEAD_DIM = 128
TOK = 128
TILES_T = 4
TILES_H = 8
MESH = pl.DeviceIdType.MESH
FAR = 1e30
LOG2E = math.log2(math.e)
SCALE = HEAD_DIM ** (-0.5)

ROW_Q, ROW_G, ROW_S, ROWS = 0, 128, 256, 272

VARIANTS = (
    (12, 0, 0), (7, 2, 2), (6, 2, 3), (5, 2, 3), (4, 2, 3), (3, 2, 3), (4, 1, 4), (4, 4, 1),
)

OFFSETS = ((0, 1), (-1, 0), (1, 1), (-1, 1), (1, 0), (0, -1), (1, -1), (-1, -1))
TERM = {6: 0, 5: 1, 7: 2, 4: 3, 2: 4, 1: 5, 0: 6, 3: 7}


def nt(a, b):
    return lax.dot_general(a, b, (((1,), (1,)), ((), ())), preferred_element_type=jnp.float32)


def nn(a, b):
    return jnp.dot(a, b, preferred_element_type=jnp.float32)


def tn(a, b):
    return lax.dot_general(a, b, (((0,), (0,)), ((), ())), preferred_element_type=jnp.float32)


def split3(x):
    hi = x.astype(jnp.bfloat16)
    rest = x - hi.astype(jnp.float32)
    mid = rest.astype(jnp.bfloat16)
    lo = (rest - mid.astype(jnp.float32)).astype(jnp.bfloat16)
    return [hi, mid, lo]


def loop(low, high, body):
    if high > low:
        lax.fori_loop(low, high, lambda i, c: (body(i), c)[1], 0)


def kernel(
    counts_abc,
    own, kv, pen, res,
    rcv11, rcv10, rcv01, out11, in11, out10, in10, out01, in01, held,
    ss11, rs11, ss10, rs10, ss01, rs01,
):
    A, B, C = counts_abc
    grp, ta, ha = lax.axis_index("grp"), lax.axis_index("ta"), lax.axis_index("ha")
    x, p = ha // 2, lax.rem(ha, 2)
    z = ta * 2 + p
    s = 1 - 2 * p

    def dev(dx, dz):
        zz = lax.rem(z + dz * s + 8, 8)
        xx = lax.rem(x + dx * s + 4, 4)
        return (grp, zz // 2, xx * 2 + lax.rem(zz, 2))

    zf, zb, xf, xb, z2f, z2b = dev(0, 1), dev(0, -1), dev(1, 0), dev(-1, 0), dev(0, 2), dev(0, -2)

    barrier = pltpu.get_barrier_semaphore()
    for d in (zf, zb, xf, xb, z2f, z2b):
        pl.semaphore_signal(barrier, inc=1, device_id=d, device_id_type=MESH)

    def remote(src, dst, ssem, rsem, to):
        return pltpu.make_async_remote_copy(
            src_ref=src, dst_ref=dst, send_sem=ssem, recv_sem=rsem, device_id=to, device_id_type=MESH
        )

    def copy11(e, t):
        src = (
            own.at[t], rcv11.at[t, 0], rcv11.at[t, 1], own.at[t],
            rcv11.at[t, 3], rcv11.at[t, 0], rcv11.at[t, 2], rcv11.at[t, 3],
        )[e]
        to = (zf, zb, zf, zb, zf, xf, xf, xf)[e]
        return remote(src, rcv11.at[t, e], ss11.at[t, e], rs11.at[t, e], to)

    def back11(i, t):
        if i == 0:
            return remote(out11.at[t, pl.ds(0, 3)], in11.at[t, pl.ds(0, 3)], ss11.at[t, 8], rs11.at[t, 8], xb)
        to = {3: zf, 4: zf, 5: zb, 6: zf, 7: zb}[i]
        return remote(out11.at[t, i], in11.at[t, i], ss11.at[t, 6 + i], rs11.at[t, 6 + i], to)

    def copy10(e, t):
        return remote(own.at[A + t], rcv10.at[t, e], ss10.at[t, e], rs10.at[t, e], (z2f, z2b)[e])

    def back10(e, t):
        return remote(out10.at[t, e], in10.at[t, e], ss10.at[t, 2 + e], rs10.at[t, 2 + e], (z2b, z2f)[e])

    def copy01(e, t):
        src = own.at[A + B + t] if e == 0 else rcv01.at[t, 0]
        return remote(src, rcv01.at[t, e], ss01.at[t, e], rs01.at[t, e], (zf, xf)[e])

    def back01(e, t):
        return remote(out01.at[t, e], in01.at[t, e], ss01.at[t, 2 + e], rs01.at[t, 2 + e], (zf, xb)[e])

    def compute(j, blocks):
        k0, v0 = kv[j, 0], kv[j, 1]
        lse_rows, delta_rows = [], []
        for ref, e in blocks:
            rows = ref[ROW_S:ROW_S + 16].astype(jnp.float32)
            lse_row = rows[0:1] + rows[1:2] + rows[2:3]
            lse_rows.append(lse_row if e is None else lse_row + pen[j, e:e + 1])
            delta_rows.append(rows[3:4] + rows[4:5] + rows[5:6])
        qs = jnp.concatenate([ref[ROW_Q:ROW_Q + TOK] for ref, _ in blocks], axis=0)
        gs = jnp.concatenate([ref[ROW_G:ROW_G + TOK] for ref, _ in blocks], axis=0)
        lse_row, delta_row = jnp.concatenate(lse_rows, axis=1), jnp.concatenate(delta_rows, axis=1)
        prob = jnp.exp2(nt(k0, qs) * (SCALE * LOG2E) - lse_row)
        ds = (prob * (nt(v0, gs) - delta_row) * SCALE).astype(jnp.bfloat16)
        res[j, 2] = nn(prob.astype(jnp.bfloat16), gs).astype(jnp.bfloat16)
        res[j, 1] = nn(ds, qs).astype(jnp.bfloat16)
        dq = tn(ds, k0)
        return [dq[i * TOK:(i + 1) * TOK] for i in range(len(blocks))]

    def f32(v):
        return v.astype(jnp.float32)

    def attend11(t):
        blocks = [(own.at[t], None)] + [(rcv11.at[t, e], e) for e in range(8)]
        parts = compute(t, blocks)
        for e in range(8):
            if TERM[e] < 4:
                out11[t, TERM[e]] = parts[1 + e].astype(jnp.bfloat16)
            else:
                held[t, TERM[e] - 4] = parts[1 + e]
        held[t, 4] = parts[0]

    pl.semaphore_wait(barrier, 6)

    def start11(t):
        copy11(0, t).start()
        copy11(3, t).start()

    loop(0, A, start11)

    def others_out():
        def start10(t):
            copy10(0, t).start()
            copy10(1, t).start()

        loop(0, B, start10)
        loop(0, C, lambda t: copy01(0, t).start())

    def plain(j):
        res[j, 0] = compute(j, [(own.at[j], None)])[0].astype(jnp.bfloat16)

    def relay01(t):
        copy01(0, t).wait_recv()
        copy01(1, t).start()

    def attend10(t):
        copy10(0, t).wait_recv()
        copy10(1, t).wait_recv()
        j = A + t
        parts = compute(j, [(own.at[j], None), (rcv10.at[t, 0], 1), (rcv10.at[t, 1], 4)])
        held[j, 4] = parts[0]
        for e in range(2):
            out10[t, e] = parts[1 + e].astype(jnp.bfloat16)
            back10(e, t).start()

    def attend01(t):
        copy01(1, t).wait_recv()
        j = A + B + t
        parts = compute(j, [(own.at[j], None), (rcv01.at[t, 0], 0), (rcv01.at[t, 1], 5)])
        held[j, 4] = parts[0]
        held[j, 2] = parts[1]
        out01[t, 1] = parts[2].astype(jnp.bfloat16)
        back01(1, t).start()

    def merge01(t):
        back01(1, t).wait_recv()
        out01[t, 0] = (held[A + B + t, 2] + f32(in01[t, 1])).astype(jnp.bfloat16)
        back01(0, t).start()

    def step(t):
        @pl.when(t < A)
        def _():
            copy11(0, t).wait_recv()
            copy11(1, t).start()
            copy11(5, t).start()
            copy11(3, t).wait_recv()
            copy11(4, t).start()
            copy11(7, t).start()

        @pl.when(t == 0)
        def _():
            others_out()

        @pl.when((t >= 1) & (t < A + 1))
        def _():
            copy11(1, t - 1).wait_recv()
            copy11(2, t - 1).start()

        @pl.when((t >= 2) & (t < A + 2))
        def _():
            copy11(2, t - 2).wait_recv()
            copy11(6, t - 2).start()

        @pl.when(t == 2)
        def _():
            loop(0, C, relay01)
            loop(A + B + C, HEADS, plain)

        @pl.when((t >= 3) & (t < A + 3))
        def _():
            u = t - 3
            for e in (4, 5, 7, 6):
                copy11(e, u).wait_recv()
            attend11(u)
            back11(0, u).start()
            back11(3, u).start()

        @pl.when(t == 3)
        def _():
            loop(0, B, attend10)
            loop(0, C, attend01)

        @pl.when((t >= 4) & (t < A + 4))
        def _():
            u = t - 4
            back11(0, u).wait_recv()
            out11[u, 4] = (held[u, 0] + f32(in11[u, 0])).astype(jnp.bfloat16)
            back11(4, u).start()
            back11(3, u).wait_recv()
            out11[u, 7] = (held[u, 3] + f32(in11[u, 2]) + f32(in11[u, 3])).astype(jnp.bfloat16)
            back11(7, u).start()

        @pl.when(t == 4)
        def _():
            loop(0, C, merge01)

        @pl.when((t >= 5) & (t < A + 5))
        def _():
            u = t - 5
            back11(4, u).wait_recv()
            out11[u, 5] = (held[u, 1] + f32(in11[u, 4])).astype(jnp.bfloat16)
            back11(5, u).start()

        @pl.when((t >= 6) & (t < A + 6))
        def _():
            u = t - 6
            back11(5, u).wait_recv()
            out11[u, 6] = (held[u, 2] + f32(in11[u, 1]) + f32(in11[u, 5])).astype(jnp.bfloat16)
            back11(6, u).start()

        @pl.when(t >= 7)
        def _():
            u = t - 7
            back11(7, u).wait_recv()
            back11(6, u).wait_recv()
            res[u, 0] = (held[u, 4] + f32(in11[u, 6]) + f32(in11[u, 7])).astype(jnp.bfloat16)

    loop(0, A + 7, step)

    def finish10(t):
        back10(0, t).wait_recv()
        back10(1, t).wait_recv()
        j = A + t
        res[j, 0] = (held[j, 4] + f32(in10[t, 0]) + f32(in10[t, 1])).astype(jnp.bfloat16)

    def finish01(t):
        back01(0, t).wait_recv()
        j = A + B + t
        res[j, 0] = (held[j, 4] + f32(in01[t, 0])).astype(jnp.bfloat16)

    loop(0, B, finish10)
    loop(0, C, finish01)

    def drain11(t):
        for e in range(8):
            copy11(e, t).wait_send()
        for i in (0, 3, 4, 5, 6, 7):
            back11(i, t).wait_send()

    def drain10(t):
        for e in range(2):
            copy10(e, t).wait_send()
            back10(e, t).wait_send()

    def drain01(t):
        for e in range(2):
            copy01(e, t).wait_send()
            back01(e, t).wait_send()

    loop(0, A, drain11)
    loop(0, B, drain10)
    loop(0, C, drain01)


def ordered(
    reach_ref, counts_ref, q_ref, k_ref, v_ref, o_ref, g_ref, lse_ref,
    choice_ref, slot_ref, own, kv, pen, perm_ref,
):
    ta, ha = lax.axis_index("ta"), lax.axis_index("ha")
    s = 1 - 2 * lax.rem(ha, 2)
    live = counts_ref[ta, ha]
    rt = [reach_ref[h, 0] for h in range(HEADS)]
    rh = [reach_ref[h, 1] for h in range(HEADS)]
    n11 = sum(t * h for t, h in zip(rt, rh))
    n10 = sum(rt) - n11
    n01 = sum(rh) - n11
    choice, A, B, C = [jnp.int32(v) for v in (0, *VARIANTS[0])]
    for i in sorted(range(len(VARIANTS)), key=lambda i: -price(VARIANTS[i])):
        a, b, c = VARIANTS[i]
        fits = n11 + jnp.maximum(n10 - b, 0) + jnp.maximum(n01 - c, 0) <= a
        choice, A, B, C = [jnp.where(fits, new, old) for new, old in zip((i, a, b, c), (choice, A, B, C))]
    choice_ref[0] = choice
    c11, c10, c01, c00 = [jnp.int32(0)] * 4
    first = []
    for h in range(HEADS):
        own10 = (rt[h] == 1) & (rh[h] == 0) & (c10 < B)
        own01 = (rt[h] == 0) & (rh[h] == 1) & (c01 < C)
        none = (rt[h] == 0) & (rh[h] == 0)
        first.append(jnp.where(none, -1, jnp.where(own10, A + c10, jnp.where(own01, A + B + c01, c11))))
        c10 = c10 + jnp.where(own10, 1, 0)
        c01 = c01 + jnp.where(own01, 1, 0)
        c11 = c11 + jnp.where(own10 | own01 | none, 0, 1)
    for h in range(HEADS):
        none = first[h] < 0
        in11 = none & (c11 < A)
        in10 = none & (c11 >= A) & (c10 < B)
        in01 = none & (c11 >= A) & (c10 >= B) & (c01 < C)
        in00 = none & (c11 >= A) & (c10 >= B) & (c01 >= C)
        slot = jnp.where(
            none,
            jnp.where(in11, c11, jnp.where(in10, A + c10, jnp.where(in01, A + B + c01, A + B + C + c00))),
            first[h],
        )
        c11, c10, c01, c00 = [
            n + jnp.where(taken, 1, 0) for n, taken in ((c11, in11), (c10, in10), (c01, in01), (c00, in00))
        ]
        slot_ref[h] = slot
        perm_ref[slot] = h
    keep = lax.broadcasted_iota(jnp.int32, (TOK, HEAD_DIM), 0) < live
    lane_ids = lax.broadcasted_iota(jnp.int32, (1, TOK), 1)
    sub_ids = lax.broadcasted_iota(jnp.int32, (8, TOK), 0)
    for j in range(HEADS):
        h = perm_ref[j]
        c = pl.ds(pl.multiple_of(h * HEAD_DIM, HEAD_DIM), HEAD_DIM)
        g = g_ref[0, 0, :, c]
        own[j, ROW_Q:ROW_Q + TOK] = q_ref[0, 0, :, c]
        own[j, ROW_G:ROW_G + TOK] = g
        kv[j, 0] = jnp.where(keep, k_ref[0, 0, :, c].astype(jnp.float32), 0.0).astype(jnp.bfloat16)
        kv[j, 1] = v_ref[0, 0, :, c]
        prod = g.astype(jnp.float32) * o_ref[0, 0, :, c].astype(jnp.float32)
        delta_row = jnp.sum(prod.T, axis=0, keepdims=True)
        lse_row = lse_ref[0, 0, pl.ds(h, 1), :] * LOG2E
        rows = split3(jnp.where(lane_ids < live, lse_row, FAR)) + split3(delta_row)
        rows = [r.astype(jnp.float32) for r in rows] + [jnp.zeros((10, TOK), jnp.float32)]
        own[j, ROW_S:ROW_S + 16] = jnp.concatenate(rows, axis=0).astype(jnp.bfloat16)
        far = jnp.zeros((8, TOK), jnp.float32)
        for e, (dt, dh) in enumerate(OFFSETS):
            at, ah = ta + dt * s, ha + dh * s
            inside = (at >= 0) & (at < TILES_T) & (ah >= 0) & (ah < TILES_H)
            seen = inside & (reach_ref[h, 0] >= abs(dt)) & (reach_ref[h, 1] >= abs(dh))
            far = jnp.where(sub_ids == e, jnp.where(seen, jnp.float32(0.0), jnp.float32(FAR)), far)
        pen[j] = far


def restored(slot_ref, counts_ref, res, dq_ref, dk_ref, dv_ref):
    live = counts_ref[lax.axis_index("ta"), lax.axis_index("ha")]
    keep = lax.broadcasted_iota(jnp.int32, (TOK, HEAD_DIM), 0) < live
    for h in range(HEADS):
        j = slot_ref[h]
        c = slice(h * HEAD_DIM, (h + 1) * HEAD_DIM)
        dq_ref[0, 0, :, c] = res[j, 0]
        for i, out in ((1, dk_ref), (2, dv_ref)):
            out[0, 0, :, c] = jnp.where(keep, res[j, i].astype(jnp.float32), 0.0).astype(jnp.bfloat16)


def price(variant):
    A, B, C = variant
    return 9 * A + 6 * B + 3 * C


VMEM, SMEM = pl.BlockSpec(memory_space=pltpu.VMEM), pl.BlockSpec(memory_space=pltpu.SMEM)
OWN = (HEADS, ROWS, HEAD_DIM)


def exchange(index, own, kv, pen):
    A, B, C = VARIANTS[index]
    dma = pltpu.SemaphoreType.DMA
    b, c = max(B, 1), max(C, 1)
    return pl.pallas_call(
        functools.partial(kernel, (A, B, C)),
        out_shape=jax.ShapeDtypeStruct((HEADS, 3, TOK, HEAD_DIM), jnp.bfloat16),
        in_specs=[VMEM] * 3,
        out_specs=VMEM,
        scratch_shapes=[
            pltpu.VMEM((A, 8, ROWS, HEAD_DIM), jnp.bfloat16),
            pltpu.VMEM((b, 2, ROWS, HEAD_DIM), jnp.bfloat16),
            pltpu.VMEM((c, 2, ROWS, HEAD_DIM), jnp.bfloat16),
            pltpu.VMEM((A, 8, TOK, HEAD_DIM), jnp.bfloat16),
            pltpu.VMEM((A, 8, TOK, HEAD_DIM), jnp.bfloat16),
            pltpu.VMEM((b, 2, TOK, HEAD_DIM), jnp.bfloat16),
            pltpu.VMEM((b, 2, TOK, HEAD_DIM), jnp.bfloat16),
            pltpu.VMEM((c, 2, TOK, HEAD_DIM), jnp.bfloat16),
            pltpu.VMEM((c, 2, TOK, HEAD_DIM), jnp.bfloat16),
            pltpu.VMEM((HEADS, 5, TOK, HEAD_DIM), jnp.float32),
            dma((A, 14)), dma((A, 14)), dma((b, 4)), dma((b, 4)), dma((c, 4)), dma((c, 4)),
        ],
        compiler_params=pltpu.CompilerParams(
            collective_id=index, has_side_effects=True, vmem_limit_bytes=56 * 2**20
        ),
        name=f"exchange_{A}_{B}_{C}",
    )(own, kv, pen)


def per_device(queries, key_tiles, value_tiles, outputs, grads_out, log_sums, tile_counts, head_reach):
    params = pltpu.CompilerParams(vmem_limit_bytes=32 * 2**20)
    choice, slots, own, kv, pen = pl.pallas_call(
        ordered,
        out_shape=(
            jax.ShapeDtypeStruct((1,), jnp.int32),
            jax.ShapeDtypeStruct((HEADS,), jnp.int32),
            jax.ShapeDtypeStruct(OWN, jnp.bfloat16),
            jax.ShapeDtypeStruct((HEADS, 2, TOK, HEAD_DIM), jnp.bfloat16),
            jax.ShapeDtypeStruct((HEADS, 8, TOK), jnp.float32),
        ),
        in_specs=[SMEM] * 2 + [VMEM] * 6,
        out_specs=(SMEM, SMEM, VMEM, VMEM, VMEM),
        scratch_shapes=[pltpu.SMEM((HEADS,), jnp.int32)],
        compiler_params=params,
        name="ordered",
    )(head_reach, tile_counts, queries, key_tiles, value_tiles, outputs, grads_out, log_sums)
    branches = [functools.partial(exchange, i) for i in range(len(VARIANTS))]
    res = branches[0](own, kv, pen) if len(branches) == 1 else lax.switch(choice[0], branches, own, kv, pen)
    tile = jax.ShapeDtypeStruct((1, 1, TOK, HEADS * HEAD_DIM), jnp.bfloat16)
    return pl.pallas_call(
        restored,
        out_shape=(tile, tile, tile),
        in_specs=[SMEM, SMEM, VMEM],
        out_specs=(VMEM, VMEM, VMEM),
        compiler_params=params,
        name="restored",
    )(slots, tile_counts, res)


def solution(mesh):
    tiles = P(("grp", "ta"), "ha", None, None)
    return jax.shard_map(
        per_device, mesh=mesh,
        in_specs=(tiles,) * 6 + (P("grp", None), P()),
        out_specs=(tiles,) * 3, check_vma=False,
    )
```

```python
import functools
import math

import jax
import jax.numpy as jnp
from jax import lax
from jax.experimental import pallas as pl
from jax.experimental.pallas import tpu as pltpu
from jax.sharding import PartitionSpec as P

HEADS = 12
HEAD_DIM = 128
TOK = 128
TILES_T = 4
TILES_H = 8
MESH = pl.DeviceIdType.MESH
FAR = 1e30
LOG2E = math.log2(math.e)
SCALE = HEAD_DIM ** (-0.5)

ROW_Q, ROW_G, ROW_S, ROWS = 0, 128, 256, 272

VARIANTS = (
    (12, 0, 0), (9, 1, 1), (7, 2, 2), (6, 2, 2), (6, 1, 4), (5, 4, 2), (5, 2, 3), (5, 1, 4),
    (4, 4, 2), (4, 3, 2), (4, 2, 3), (4, 1, 4), (3, 3, 2), (3, 2, 3), (3, 1, 4), (2, 2, 3),
)

OFFSETS = ((0, 1), (-1, 0), (1, 1), (-1, 1), (1, 0), (0, -1), (1, -1), (-1, -1))
TERM = {6: 0, 5: 1, 7: 2, 4: 3, 2: 4, 1: 5, 0: 6, 3: 7}


def nt(a, b):
    return lax.dot_general(a, b, (((1,), (1,)), ((), ())), preferred_element_type=jnp.float32)


def nn(a, b):
    return jnp.dot(a, b, preferred_element_type=jnp.float32)


def tn(a, b):
    return lax.dot_general(a, b, (((0,), (0,)), ((), ())), preferred_element_type=jnp.float32)


def split3(x):
    hi = x.astype(jnp.bfloat16)
    rest = x - hi.astype(jnp.float32)
    mid = rest.astype(jnp.bfloat16)
    lo = (rest - mid.astype(jnp.float32)).astype(jnp.bfloat16)
    return [hi, mid, lo]


def loop(low, high, body):
    if high > low:
        lax.fori_loop(low, high, lambda i, c: (body(i), c)[1], 0)


def schedule(A, B, C):
    out = min(A, 3)
    return dict(ahead=3, out=out, relay=out + 1, work=out + 2, merge=out + 3, hopf=1, hopb=1)


def kernel(
    counts_abc,
    plan,
    own, kv, pen, res,
    rcv11, rcv10, rcv01, out11, in11, out10, in10, out01, in01, held,
    ss11, rs11, ss10, rs10, ss01, rs01,
):
    A, B, C = counts_abc
    grp, ta, ha = lax.axis_index("grp"), lax.axis_index("ta"), lax.axis_index("ha")
    x, p = ha // 2, lax.rem(ha, 2)
    z = ta * 2 + p
    s = 1 - 2 * p

    def dev(dx, dz):
        zz = lax.rem(z + dz * s + 8, 8)
        xx = lax.rem(x + dx * s + 4, 4)
        return (grp, zz // 2, xx * 2 + lax.rem(zz, 2))

    zf, zb, xf, xb, z2f, z2b = dev(0, 1), dev(0, -1), dev(1, 0), dev(-1, 0), dev(0, 2), dev(0, -2)

    barrier = pltpu.get_barrier_semaphore()
    for d in (zf, zb, xf, xb, z2f, z2b):
        pl.semaphore_signal(barrier, inc=1, device_id=d, device_id_type=MESH)

    far_out, far_back = plan["hopf"], plan["hopb"]
    lag = 2 if far_out else 3
    last = lag + (3 if far_back else 4)

    def remote(src, dst, ssem, rsem, to):
        return pltpu.make_async_remote_copy(
            src_ref=src, dst_ref=dst, send_sem=ssem, recv_sem=rsem, device_id=to, device_id_type=MESH
        )

    def copy11(e, t):
        src = (
            own.at[t], rcv11.at[t, 0], rcv11.at[t, 0 if far_out else 1], own.at[t],
            rcv11.at[t, 3], rcv11.at[t, 0], rcv11.at[t, 2], rcv11.at[t, 3],
        )[e]
        to = (zf, zb, z2b if far_out else zf, zb, zf, xf, xf, xf)[e]
        return remote(src, rcv11.at[t, e], ss11.at[t, e], rs11.at[t, e], to)

    def back11(i, t):
        if i == 0:
            return remote(out11.at[t, pl.ds(0, 3)], in11.at[t, pl.ds(0, 3)], ss11.at[t, 8], rs11.at[t, 8], xb)
        to = {3: zf, 4: z2f if far_back else zf, 5: zb, 6: zf, 7: zb}[i]
        return remote(out11.at[t, i], in11.at[t, i], ss11.at[t, 6 + i], rs11.at[t, 6 + i], to)

    def copy10(e, t):
        return remote(own.at[A + t], rcv10.at[t, e], ss10.at[t, e], rs10.at[t, e], (z2f, z2b)[e])

    def back10(e, t):
        return remote(out10.at[t, e], in10.at[t, e], ss10.at[t, 2 + e], rs10.at[t, 2 + e], (z2b, z2f)[e])

    def copy01(e, t):
        src = own.at[A + B + t] if e == 0 else rcv01.at[t, 0]
        return remote(src, rcv01.at[t, e], ss01.at[t, e], rs01.at[t, e], (zf, xf)[e])

    def back01(e, t):
        return remote(out01.at[t, e], in01.at[t, e], ss01.at[t, 2 + e], rs01.at[t, 2 + e], (zf, xb)[e])

    def compute(j, blocks):
        k0, v0 = kv[j, 0], kv[j, 1]
        lse_rows, delta_rows = [], []
        for ref, e in blocks:
            rows = ref[ROW_S:ROW_S + 16].astype(jnp.float32)
            lse_row = rows[0:1] + rows[1:2] + rows[2:3]
            lse_rows.append(lse_row if e is None else lse_row + pen[j, e:e + 1])
            delta_rows.append(rows[3:4] + rows[4:5] + rows[5:6])
        qs = jnp.concatenate([ref[ROW_Q:ROW_Q + TOK] for ref, _ in blocks], axis=0)
        gs = jnp.concatenate([ref[ROW_G:ROW_G + TOK] for ref, _ in blocks], axis=0)
        lse_row, delta_row = jnp.concatenate(lse_rows, axis=1), jnp.concatenate(delta_rows, axis=1)
        prob = jnp.exp2(nt(k0, qs) * (SCALE * LOG2E) - lse_row)
        ds = (prob * (nt(v0, gs) - delta_row) * SCALE).astype(jnp.bfloat16)
        res[j, 2] = nn(prob.astype(jnp.bfloat16), gs).astype(jnp.bfloat16)
        res[j, 1] = nn(ds, qs).astype(jnp.bfloat16)
        dq = tn(ds, k0)
        return [dq[i * TOK:(i + 1) * TOK] for i in range(len(blocks))]

    def f32(v):
        return v.astype(jnp.float32)

    def attend11(t):
        blocks = [(own.at[t], None)] + [(rcv11.at[t, e], e) for e in range(8)]
        parts = compute(t, blocks)
        for e in range(8):
            if TERM[e] < 4 or (far_back and TERM[e] == 5):
                out11[t, TERM[e]] = parts[1 + e].astype(jnp.bfloat16)
            else:
                held[t, TERM[e] - 4] = parts[1 + e]
        held[t, 4] = parts[0]

    def plain(j):
        res[j, 0] = compute(j, [(own.at[j], None)])[0].astype(jnp.bfloat16)

    loop(A + B + C, HEADS, plain)
    pl.semaphore_wait(barrier, 6)

    def start11(t):
        copy11(0, t).start()
        copy11(3, t).start()

    ahead = min(A, plan["ahead"])
    loop(0, ahead, start11)

    def others_out():
        def start10(t):
            copy10(0, t).start()
            copy10(1, t).start()

        loop(0, B, start10)
        loop(0, C, lambda t: copy01(0, t).start())

    def relay01(t):
        copy01(0, t).wait_recv()
        copy01(1, t).start()

    def attend10(t):
        copy10(0, t).wait_recv()
        copy10(1, t).wait_recv()
        j = A + t
        parts = compute(j, [(own.at[j], None), (rcv10.at[t, 0], 1), (rcv10.at[t, 1], 4)])
        held[j, 4] = parts[0]
        for e in range(2):
            out10[t, e] = parts[1 + e].astype(jnp.bfloat16)
            back10(e, t).start()

    def attend01(t):
        copy01(1, t).wait_recv()
        j = A + B + t
        parts = compute(j, [(own.at[j], None), (rcv01.at[t, 0], 0), (rcv01.at[t, 1], 5)])
        held[j, 4] = parts[0]
        held[j, 2] = parts[1]
        out01[t, 1] = parts[2].astype(jnp.bfloat16)
        back01(1, t).start()

    def merge01(t):
        back01(1, t).wait_recv()
        out01[t, 0] = (held[A + B + t, 2] + f32(in01[t, 1])).astype(jnp.bfloat16)
        back01(0, t).start()

    def step(t):
        if ahead < A:
            @pl.when(t < A - ahead)
            def _():
                start11(t + ahead)

        @pl.when(t < A)
        def _():
            copy11(0, t).wait_recv()
            if far_out:
                copy11(2, t).start()
            copy11(1, t).start()
            copy11(5, t).start()
            copy11(3, t).wait_recv()
            copy11(4, t).start()
            copy11(7, t).start()

        @pl.when(t == plan["out"])
        def _():
            others_out()

        if not far_out:
            @pl.when((t >= 1) & (t < A + 1))
            def _():
                copy11(1, t - 1).wait_recv()
                copy11(2, t - 1).start()

        @pl.when((t >= lag - 1) & (t < A + lag - 1))
        def _():
            copy11(2, t - lag + 1).wait_recv()
            copy11(6, t - lag + 1).start()

        @pl.when(t == plan["relay"])
        def _():
            loop(0, C, relay01)

        @pl.when((t >= lag) & (t < A + lag))
        def _():
            u = t - lag
            for e in (1, 4, 5, 7, 6) if far_out else (4, 5, 7, 6):
                copy11(e, u).wait_recv()
            attend11(u)
            back11(0, u).start()
            back11(3, u).start()
            if far_back:
                back11(5, u).start()

        @pl.when(t == plan["work"])
        def _():
            loop(0, B, attend10)
            loop(0, C, attend01)

        @pl.when((t >= lag + 1) & (t < A + lag + 1))
        def _():
            u = t - lag - 1
            back11(0, u).wait_recv()
            out11[u, 4] = (held[u, 0] + f32(in11[u, 0])).astype(jnp.bfloat16)
            back11(4, u).start()
            back11(3, u).wait_recv()
            out11[u, 7] = (held[u, 3] + f32(in11[u, 2]) + f32(in11[u, 3])).astype(jnp.bfloat16)
            back11(7, u).start()

        @pl.when(t == plan["merge"])
        def _():
            loop(0, C, merge01)

        if not far_back:
            @pl.when((t >= lag + 2) & (t < A + lag + 2))
            def _():
                u = t - lag - 2
                back11(4, u).wait_recv()
                out11[u, 5] = (held[u, 1] + f32(in11[u, 4])).astype(jnp.bfloat16)
                back11(5, u).start()

        @pl.when((t >= last - 1) & (t < A + last - 1))
        def _():
            u = t - last + 1
            term = held[u, 2] + f32(in11[u, 1])
            back11(5, u).wait_recv()
            if far_back:
                back11(4, u).wait_recv()
                term = term + f32(in11[u, 4])
            out11[u, 6] = (term + f32(in11[u, 5])).astype(jnp.bfloat16)
            back11(6, u).start()

        @pl.when(t >= last)
        def _():
            u = t - last
            back11(7, u).wait_recv()
            back11(6, u).wait_recv()
            res[u, 0] = (held[u, 4] + f32(in11[u, 6]) + f32(in11[u, 7])).astype(jnp.bfloat16)

    loop(0, A + last, step)

    def finish10(t):
        back10(0, t).wait_recv()
        back10(1, t).wait_recv()
        j = A + t
        res[j, 0] = (held[j, 4] + f32(in10[t, 0]) + f32(in10[t, 1])).astype(jnp.bfloat16)

    def finish01(t):
        back01(0, t).wait_recv()
        j = A + B + t
        res[j, 0] = (held[j, 4] + f32(in01[t, 0])).astype(jnp.bfloat16)

    loop(0, B, finish10)
    loop(0, C, finish01)

    def drain11(t):
        for e in range(8):
            copy11(e, t).wait_send()
        for i in (0, 3, 4, 5, 6, 7):
            back11(i, t).wait_send()

    def drain10(t):
        for e in range(2):
            copy10(e, t).wait_send()
            back10(e, t).wait_send()

    def drain01(t):
        for e in range(2):
            copy01(e, t).wait_send()
            back01(e, t).wait_send()

    loop(0, A, drain11)
    loop(0, B, drain10)
    loop(0, C, drain01)


def ordered(
    reach_ref, counts_ref, q_ref, k_ref, v_ref, o_ref, g_ref, lse_ref,
    choice_ref, slot_ref, own, kv, pen,
    perm_ref, q_all, k_all, v_all, o_all, g_all, lse_all, stats, sems,
):
    loads = [
        pltpu.make_async_copy(src, dst, sems.at[i])
        for i, (src, dst) in enumerate((
            (lse_ref, lse_all), (g_ref.at[0, 0], g_all), (o_ref.at[0, 0], o_all),
            (q_ref.at[0, 0], q_all), (k_ref.at[0, 0], k_all), (v_ref.at[0, 0], v_all),
        ))
    ]
    for load in loads:
        load.start()
    ta, ha = lax.axis_index("ta"), lax.axis_index("ha")
    s = 1 - 2 * lax.rem(ha, 2)
    live = counts_ref[ta, ha]
    rt = [reach_ref[0, h] for h in range(HEADS)]
    rh = [reach_ref[1, h] for h in range(HEADS)]
    n11 = sum(t * h for t, h in zip(rt, rh))
    n10 = sum(rt) - n11
    n01 = sum(rh) - n11
    choice, A, B, C = [jnp.int32(v) for v in (0, *VARIANTS[0])]
    for i in sorted(range(len(VARIANTS)), key=lambda i: -price(VARIANTS[i])):
        a, b, c = VARIANTS[i]
        fits = n11 + jnp.maximum(n10 - b, 0) + jnp.maximum(n01 - c, 0) <= a
        choice, A, B, C = [jnp.where(fits, new, old) for new, old in zip((i, a, b, c), (choice, A, B, C))]
    choice_ref[0] = choice
    c11, c10, c01, c00 = [jnp.int32(0)] * 4
    first = []
    for h in range(HEADS):
        own10 = (rt[h] == 1) & (rh[h] == 0) & (c10 < B)
        own01 = (rt[h] == 0) & (rh[h] == 1) & (c01 < C)
        none = (rt[h] == 0) & (rh[h] == 0)
        first.append(jnp.where(none, -1, jnp.where(own10, A + c10, jnp.where(own01, A + B + c01, c11))))
        c10 = c10 + jnp.where(own10, 1, 0)
        c01 = c01 + jnp.where(own01, 1, 0)
        c11 = c11 + jnp.where(own10 | own01 | none, 0, 1)
    for h in range(HEADS):
        none = first[h] < 0
        in11 = none & (c11 < A)
        in10 = none & (c11 >= A) & (c10 < B)
        in01 = none & (c11 >= A) & (c10 >= B) & (c01 < C)
        in00 = none & (c11 >= A) & (c10 >= B) & (c01 >= C)
        slot = jnp.where(
            none,
            jnp.where(in11, c11, jnp.where(in10, A + c10, jnp.where(in01, A + B + c01, A + B + C + c00))),
            first[h],
        )
        c11, c10, c01, c00 = [
            n + jnp.where(taken, 1, 0) for n, taken in ((c11, in11), (c10, in10), (c01, in01), (c00, in00))
        ]
        slot_ref[h] = slot
        perm_ref[slot] = h
    keep = lax.broadcasted_iota(jnp.int32, (TOK, HEAD_DIM), 0) < live
    lane_ids = lax.broadcasted_iota(jnp.int32, (1, TOK), 1)
    sub_ids = lax.broadcasted_iota(jnp.int32, (8, TOK), 0)
    for load in loads[:3]:
        load.wait()
    feature = lax.broadcasted_iota(jnp.int32, (16, HEADS * HEAD_DIM), 1) // HEAD_DIM
    member = jnp.where(feature == lax.broadcasted_iota(jnp.int32, (16, HEADS * HEAD_DIM), 0), 1.0, 0.0)
    member = member.astype(jnp.bfloat16)
    prod = g_all[...].astype(jnp.float32) * o_all[...].astype(jnp.float32)
    high = prod.astype(jnp.bfloat16)
    low = (prod - high.astype(jnp.float32)).astype(jnp.bfloat16)
    delta = nt(member, high) + nt(member, low)
    delta_pieces = [p.astype(jnp.float32) for p in split3(delta)]
    stats[...] = jnp.zeros_like(stats)
    for h in range(HEADS):
        lse_row = jnp.where(lane_ids < live, lse_all[h] * LOG2E, FAR)
        for i, p in enumerate(split3(lse_row)):
            stats[h, i:i + 1] = p.astype(jnp.float32)
        for i, p in enumerate(delta_pieces):
            stats[h, 3 + i:4 + i] = p[h:h + 1]
    for load in loads[3:]:
        load.wait()
    for j in range(HEADS):
        h = perm_ref[j]
        c = pl.ds(pl.multiple_of(h * HEAD_DIM, HEAD_DIM), HEAD_DIM)
        g = g_all[:, c]
        own[j, ROW_Q:ROW_Q + TOK] = q_all[:, c]
        own[j, ROW_G:ROW_G + TOK] = g
        kv[j, 0] = jnp.where(keep, k_all[:, c].astype(jnp.float32), 0.0).astype(jnp.bfloat16)
        kv[j, 1] = v_all[:, c]
        own[j, ROW_S:ROW_S + 16] = stats[h].astype(jnp.bfloat16)
        far = jnp.zeros((8, TOK), jnp.float32)
        for e, (dt, dh) in enumerate(OFFSETS):
            at, ah = ta + dt * s, ha + dh * s
            inside = (at >= 0) & (at < TILES_T) & (ah >= 0) & (ah < TILES_H)
            seen = inside & (reach_ref[0, h] >= abs(dt)) & (reach_ref[1, h] >= abs(dh))
            far = jnp.where(sub_ids == e, jnp.where(seen, jnp.float32(0.0), jnp.float32(FAR)), far)
        pen[j] = far


def restored(slot_ref, counts_ref, res, dq_ref, dk_ref, dv_ref):
    live = counts_ref[lax.axis_index("ta"), lax.axis_index("ha")]
    keep = lax.broadcasted_iota(jnp.int32, (TOK, HEAD_DIM), 0) < live
    for h in range(HEADS):
        j = slot_ref[h]
        c = slice(h * HEAD_DIM, (h + 1) * HEAD_DIM)
        dq_ref[0, 0, :, c] = res[j, 0]
        for i, out in ((1, dk_ref), (2, dv_ref)):
            out[0, 0, :, c] = jnp.where(keep, res[j, i].astype(jnp.float32), 0.0).astype(jnp.bfloat16)


def price(variant):
    A, B, C = variant
    return 9 * A + 6 * B + 3 * C


VMEM, SMEM = pl.BlockSpec(memory_space=pltpu.VMEM), pl.BlockSpec(memory_space=pltpu.SMEM)
OWN = (HEADS, ROWS, HEAD_DIM)


def exchange(index, own, kv, pen):
    A, B, C = VARIANTS[index]
    steps = schedule(A, B, C)
    dma = pltpu.SemaphoreType.DMA
    b, c = max(B, 1), max(C, 1)
    return pl.pallas_call(
        functools.partial(kernel, (A, B, C), steps),
        out_shape=jax.ShapeDtypeStruct((HEADS, 3, TOK, HEAD_DIM), jnp.bfloat16),
        in_specs=[VMEM] * 3,
        out_specs=VMEM,
        scratch_shapes=[
            pltpu.VMEM((A, 8, ROWS, HEAD_DIM), jnp.bfloat16),
            pltpu.VMEM((b, 2, ROWS, HEAD_DIM), jnp.bfloat16),
            pltpu.VMEM((c, 2, ROWS, HEAD_DIM), jnp.bfloat16),
            pltpu.VMEM((A, 8, TOK, HEAD_DIM), jnp.bfloat16),
            pltpu.VMEM((A, 8, TOK, HEAD_DIM), jnp.bfloat16),
            pltpu.VMEM((b, 2, TOK, HEAD_DIM), jnp.bfloat16),
            pltpu.VMEM((b, 2, TOK, HEAD_DIM), jnp.bfloat16),
            pltpu.VMEM((c, 2, TOK, HEAD_DIM), jnp.bfloat16),
            pltpu.VMEM((c, 2, TOK, HEAD_DIM), jnp.bfloat16),
            pltpu.VMEM((HEADS, 5, TOK, HEAD_DIM), jnp.float32),
            dma((A, 14)), dma((A, 14)), dma((b, 4)), dma((b, 4)), dma((c, 4)), dma((c, 4)),
        ],
        compiler_params=pltpu.CompilerParams(
            collective_id=index, has_side_effects=True, vmem_limit_bytes=56 * 2**20
        ),
        name=f"exchange_{A}_{B}_{C}",
    )(own, kv, pen)


def per_device(queries, key_tiles, value_tiles, outputs, grads_out, log_sums, tile_counts, head_reach):
    params = pltpu.CompilerParams(vmem_limit_bytes=32 * 2**20)
    choice, slots, own, kv, pen = pl.pallas_call(
        ordered,
        out_shape=(
            jax.ShapeDtypeStruct((1,), jnp.int32),
            jax.ShapeDtypeStruct((HEADS,), jnp.int32),
            jax.ShapeDtypeStruct(OWN, jnp.bfloat16),
            jax.ShapeDtypeStruct((HEADS, 2, TOK, HEAD_DIM), jnp.bfloat16),
            jax.ShapeDtypeStruct((HEADS, 8, TOK), jnp.float32),
        ),
        in_specs=[SMEM] * 2 + [pl.BlockSpec(memory_space=pl.ANY)] * 6,
        out_specs=(SMEM, SMEM, VMEM, VMEM, VMEM),
        scratch_shapes=[pltpu.SMEM((HEADS,), jnp.int32)]
        + [pltpu.VMEM((TOK, HEADS * HEAD_DIM), jnp.bfloat16)] * 5
        + [pltpu.VMEM((HEADS, 1, TOK), jnp.float32), pltpu.VMEM((HEADS, 16, TOK), jnp.float32), pltpu.SemaphoreType.DMA((6,))],
        compiler_params=pltpu.CompilerParams(vmem_limit_bytes=60 * 2**20),
        name="ordered",
    )(
        head_reach.T, tile_counts, queries, key_tiles, value_tiles, outputs, grads_out,
        jnp.transpose(log_sums, (0, 2, 1, 3)).reshape(HEADS, 1, TOK),
    )
    branches = [functools.partial(exchange, i) for i in range(len(VARIANTS))]
    res = branches[0](own, kv, pen) if len(branches) == 1 else lax.switch(choice[0], branches, own, kv, pen)
    tile = jax.ShapeDtypeStruct((1, 1, TOK, HEADS * HEAD_DIM), jnp.bfloat16)
    return pl.pallas_call(
        restored,
        out_shape=(tile, tile, tile),
        in_specs=[SMEM, SMEM, VMEM],
        out_specs=(VMEM, VMEM, VMEM),
        compiler_params=params,
        name="restored",
    )(slots, tile_counts, res)


def solution(mesh):
    tiles = P(("grp", "ta"), "ha", None, None)
    return jax.shard_map(
        per_device, mesh=mesh,
        in_specs=(tiles,) * 6 + (P("grp", None), P()),
        out_specs=(tiles,) * 3, check_vma=False,
    )
```

```python
import functools
import math

import jax
import jax.numpy as jnp
from jax import lax
from jax.experimental import pallas as pl
from jax.experimental.pallas import tpu as pltpu
from jax.sharding import PartitionSpec as P

HEADS = 12
OUT01 = 1
HEAD_DIM = 128
TOK = 128
TILES_T = 4
TILES_H = 8
MESH = pl.DeviceIdType.MESH
FAR = 1e30
LOG2E = math.log2(math.e)
SCALE = HEAD_DIM ** (-0.5)

ROW_Q, ROW_G, ROW_S, ROWS = 0, 128, 256, 272

VARIANTS = (
    (12, 0), (9, 2), (8, 2), (7, 4), (7, 2), (6, 4), (6, 3), (6, 2), (5, 4), (5, 2), (4, 4), (4, 2),
)

PAIRS = (
    ((-1, 1), (-1, 1)), ((-1, 0), (-1, 0)), ((-1, -1), (-1, -1)),
    ((0, 0), (0, -1)), ((-1, 1), (-1, 0)), ((-1, 0), (-1, -1)), ((0, 2), (0, 1)), ((-1, 2), (-1, 1)),
    ((0, 1), (0, 1)), ((0, -1), (0, -1)),
)
PEN_ROWS = 16


def nt(a, b):
    return lax.dot_general(a, b, (((1,), (1,)), ((), ())), preferred_element_type=jnp.float32)


def nn(a, b):
    return jnp.dot(a, b, preferred_element_type=jnp.float32)


def tn(a, b):
    return lax.dot_general(a, b, (((0,), (0,)), ((), ())), preferred_element_type=jnp.float32)


def split3(x):
    hi = x.astype(jnp.bfloat16)
    rest = x - hi.astype(jnp.float32)
    mid = rest.astype(jnp.bfloat16)
    lo = (rest - mid.astype(jnp.float32)).astype(jnp.bfloat16)
    return [hi, mid, lo]


def loop(low, high, body):
    if high > low:
        lax.fori_loop(low, high, lambda i, c: (body(i), c)[1], 0)


def kernel(
    counts,
    own, kv, pen, res,
    rkv, rq, rq01, oq, iq, ogr, igr, o01, i01, held,
    ss, rs, ss01, rs01,
):
    A, C = counts
    grp, ta, ha = lax.axis_index("grp"), lax.axis_index("ta"), lax.axis_index("ha")
    x, p = ha // 2, lax.rem(ha, 2)
    z = ta * 2 + p
    s = 1 - 2 * p

    def dev(dx, dz):
        zz = lax.rem(z + dz * s + 8, 8)
        xx = lax.rem(x + dx * s + 4, 4)
        return (grp, zz // 2, xx * 2 + lax.rem(zz, 2))

    zf, zb, xf, xb, z2f, z2b = dev(0, 1), dev(0, -1), dev(1, 0), dev(-1, 0), dev(0, 2), dev(0, -2)

    barrier = pltpu.get_barrier_semaphore()
    for d in (zf, zb, xf, xb, z2f, z2b):
        pl.semaphore_signal(barrier, inc=1, device_id=d, device_id_type=MESH)

    def remote(src, dst, ssem, rsem, to):
        return pltpu.make_async_remote_copy(
            src_ref=src, dst_ref=dst, send_sem=ssem, recv_sem=rsem, device_id=to, device_id_type=MESH
        )

    def copy(i, t):
        src, dst, to = (
            (kv.at[t], rkv.at[t], zf),
            (own.at[t], rq.at[t, 0], zb),
            (own.at[t], rq.at[t, 1], z2f),
            (own.at[t], rq.at[t, 2], xb),
            (rq.at[t, 1], rq.at[t, 3], xb),
            (rq.at[t, 0], rq.at[t, 4], xf),
        )[i]
        return remote(src, dst, ss.at[t, i], rs.at[t, i], to)

    def back(i, t):
        src, dst, to = (
            (oq.at[t, pl.ds(0, 2)], iq.at[t, pl.ds(0, 2)], xf),
            (oq.at[t, 2], iq.at[t, 2], xb),
            (oq.at[t, 3], iq.at[t, 3], zb),
            (oq.at[t, 4], iq.at[t, 4], z2b),
            (ogr.at[t], igr.at[t], zf),
        )[i]
        return remote(src, dst, ss.at[t, 6 + i], rs.at[t, 6 + i], to)

    def copy01(e, t):
        src = own.at[A + t] if e == 0 else rq01.at[t, 0]
        return remote(src, rq01.at[t, e], ss01.at[t, e], rs01.at[t, e], (zf, xf)[e])

    def back01(e, t):
        return remote(o01.at[t, e], i01.at[t, e], ss01.at[t, 2 + e], rs01.at[t, 2 + e], (zf, xb)[e])

    def attend(j, keys, blocks):
        k0, v0 = keys[0], keys[1]
        lse_rows, delta_rows = [], []
        for ref, row in blocks:
            rows = ref[ROW_S:ROW_S + 16].astype(jnp.float32)
            lse_row = rows[0:1] + rows[1:2] + rows[2:3]
            lse_rows.append(lse_row if row is None else lse_row + pen[j, row:row + 1])
            delta_rows.append(rows[3:4] + rows[4:5] + rows[5:6])
        qs = jnp.concatenate([ref[ROW_Q:ROW_Q + TOK] for ref, _ in blocks], axis=0)
        gs = jnp.concatenate([ref[ROW_G:ROW_G + TOK] for ref, _ in blocks], axis=0)
        lse_row, delta_row = jnp.concatenate(lse_rows, axis=1), jnp.concatenate(delta_rows, axis=1)
        prob = jnp.exp2(nt(k0, qs) * (SCALE * LOG2E) - lse_row)
        ds = (prob * (nt(v0, gs) - delta_row) * SCALE).astype(jnp.bfloat16)
        dv = nn(prob.astype(jnp.bfloat16), gs)
        dk = nn(ds, qs)
        dq = tn(ds, k0)
        return dk, dv, [dq[i * TOK:(i + 1) * TOK] for i in range(len(blocks))]

    def bf16(v):
        return v.astype(jnp.bfloat16)

    def f32(v):
        return v.astype(jnp.float32)

    def plain(j):
        dk, dv, dq = attend(j, kv.at[j], [(own.at[j], None)])
        res[j, 0], res[j, 1], res[j, 2] = bf16(dq[0]), bf16(dk), bf16(dv)

    loop(A + C, HEADS, plain)
    pl.semaphore_wait(barrier, 6)

    def start(t):
        for i in (2, 1, 0, 3):
            copy(i, t).start()

    def relay01(t):
        copy01(0, t).wait_recv()
        copy01(1, t).start()

    def attend01(t):
        copy01(1, t).wait_recv()
        j = A + t
        dk, dv, dq = attend(j, kv.at[j], [(own.at[j], None), (rq01.at[t, 0], 8), (rq01.at[t, 1], 9)])
        res[j, 1], res[j, 2] = bf16(dk), bf16(dv)
        o01[t, 1] = bf16(dq[2])
        back01(1, t).start()
        held[j, 0] = dq[0]
        held[j, 1] = dq[1]

    def merge01(t):
        back01(1, t).wait_recv()
        o01[t, 0] = bf16(held[A + t, 1] + f32(i01[t, 1]))
        back01(0, t).start()

    ahead = min(A, 2 if A > 4 else 3)
    loop(0, ahead, start)

    def step(t):
        if ahead < A:
            @pl.when(t < A - ahead)
            def _():
                start(t + ahead)

        @pl.when(t < A)
        def _():
            copy(2, t).wait_recv()
            copy(4, t).start()
            copy(1, t).wait_recv()
            copy(5, t).start()

        @pl.when(t == OUT01)
        def _():
            loop(0, C, lambda i: copy01(0, i).start())

        @pl.when(t == OUT01 + 1)
        def _():
            loop(0, C, relay01)

        @pl.when((t >= 1) & (t < A + 1))
        def _():
            u = t - 1
            for i in (0, 3, 5, 4):
                copy(i, u).wait_recv()
            tiles = [rq.at[u, i] for i in range(5)]
            dk, dv, dq = attend(
                u, rkv.at[u],
                [(own.at[u], 3), (tiles[0], 4), (tiles[1], 5), (tiles[2], 6), (tiles[3], 7)],
            )
            oq[u, 0] = bf16(dq[3])
            oq[u, 1] = bf16(dq[4])
            back(0, u).start()
            ogr[u, 0] = bf16(dk)
            ogr[u, 1] = bf16(dv)
            back(4, u).start()
            for i in range(3):
                held[u, i] = dq[i]
            dk, dv, dq = attend(
                u, kv.at[u], [(own.at[u], None), (tiles[0], 0), (tiles[1], 1), (tiles[4], 2)]
            )
            oq[u, 2] = bf16(dq[3])
            back(1, u).start()
            for i in range(3):
                held[u, i] = held[u, i] + dq[i]
            held[u, 3] = dk
            held[u, 4] = dv

        @pl.when(t == OUT01 + 2)
        def _():
            loop(0, C, attend01)

        @pl.when((t >= 2) & (t < A + 2))
        def _():
            u = t - 2
            back(0, u).wait_recv()
            oq[u, 4] = bf16(held[u, 2] + f32(iq[u, 1]))
            back(3, u).start()
            back(1, u).wait_recv()
            oq[u, 3] = bf16(held[u, 1] + f32(iq[u, 2]))
            back(2, u).start()

        @pl.when(t == OUT01 + 3)
        def _():
            loop(0, C, merge01)

        @pl.when(t >= 3)
        def _():
            u = t - 3
            back(4, u).wait_recv()
            res[u, 1] = bf16(held[u, 3] + f32(igr[u, 0]))
            res[u, 2] = bf16(held[u, 4] + f32(igr[u, 1]))
            back(2, u).wait_recv()
            back(3, u).wait_recv()
            res[u, 0] = bf16(held[u, 0] + f32(iq[u, 0]) + f32(iq[u, 3]) + f32(iq[u, 4]))

    loop(0, A + 3, step)

    def finish01(t):
        back01(0, t).wait_recv()
        res[A + t, 0] = bf16(held[A + t, 0] + f32(i01[t, 0]))

    loop(0, C, finish01)

    def drain(t):
        for i in range(6):
            copy(i, t).wait_send()
        for i in range(5):
            back(i, t).wait_send()

    def drain01(t):
        for e in range(2):
            copy01(e, t).wait_send()
            back01(e, t).wait_send()

    loop(0, A, drain)
    loop(0, C, drain01)


def ordered(
    reach_ref, counts_ref, q_ref, k_ref, v_ref, o_ref, g_ref, lse_ref,
    choice_ref, slot_ref, own, kv, pen,
    perm_ref, q_all, k_all, v_all, o_all, g_all, lse_all, stats, sems,
):
    loads = [
        pltpu.make_async_copy(src, dst, sems.at[i])
        for i, (src, dst) in enumerate((
            (lse_ref, lse_all), (g_ref.at[0, 0], g_all), (o_ref.at[0, 0], o_all),
            (q_ref.at[0, 0], q_all), (k_ref.at[0, 0], k_all), (v_ref.at[0, 0], v_all),
        ))
    ]
    for load in loads:
        load.start()
    ta, ha = lax.axis_index("ta"), lax.axis_index("ha")
    s = 1 - 2 * lax.rem(ha, 2)
    live = counts_ref[ta, ha]
    rt = [reach_ref[0, h] for h in range(HEADS)]
    rh = [reach_ref[1, h] for h in range(HEADS)]
    n1 = sum(rt)
    n01 = sum(rh) - sum(t * h for t, h in zip(rt, rh))
    choice, A, C = [jnp.int32(v) for v in (0, *VARIANTS[0])]
    for i in sorted(range(len(VARIANTS)), key=lambda i: -price(VARIANTS[i])):
        a, c = VARIANTS[i]
        fits = n1 + jnp.maximum(n01 - c, 0) <= a
        choice, A, C = [jnp.where(fits, new, old) for new, old in zip((i, a, c), (choice, A, C))]
    choice_ref[0] = choice
    c1, c01, c00 = [jnp.int32(0)] * 3
    first = []
    for h in range(HEADS):
        own01 = (rt[h] == 0) & (rh[h] == 1) & (c01 < C)
        none = (rt[h] == 0) & (rh[h] == 0)
        first.append(jnp.where(none, -1, jnp.where(own01, A + c01, c1)))
        c01 = c01 + jnp.where(own01, 1, 0)
        c1 = c1 + jnp.where(own01 | none, 0, 1)
    for h in range(HEADS):
        none = first[h] < 0
        in1 = none & (c1 < A)
        in01 = none & (c1 >= A) & (c01 < C)
        in00 = none & (c1 >= A) & (c01 >= C)
        slot = jnp.where(none, jnp.where(in1, c1, jnp.where(in01, A + c01, A + C + c00)), first[h])
        c1, c01, c00 = [n + jnp.where(taken, 1, 0) for n, taken in ((c1, in1), (c01, in01), (c00, in00))]
        slot_ref[h] = slot
        perm_ref[slot] = h
    keep = lax.broadcasted_iota(jnp.int32, (TOK, HEAD_DIM), 0) < live
    lane_ids = lax.broadcasted_iota(jnp.int32, (1, TOK), 1)
    sub_ids = lax.broadcasted_iota(jnp.int32, (PEN_ROWS, TOK), 0)
    for load in loads[:3]:
        load.wait()
    feature = lax.broadcasted_iota(jnp.int32, (16, HEADS * HEAD_DIM), 1) // HEAD_DIM
    member = jnp.where(feature == lax.broadcasted_iota(jnp.int32, (16, HEADS * HEAD_DIM), 0), 1.0, 0.0)
    member = member.astype(jnp.bfloat16)
    prod = g_all[...].astype(jnp.float32) * o_all[...].astype(jnp.float32)
    high = prod.astype(jnp.bfloat16)
    low = (prod - high.astype(jnp.float32)).astype(jnp.bfloat16)
    delta = nt(member, high) + nt(member, low)
    delta_pieces = [p.astype(jnp.float32) for p in split3(delta)]
    stats[...] = jnp.zeros_like(stats)
    for h in range(HEADS):
        lse_row = jnp.where(lane_ids < live, lse_all[h] * LOG2E, FAR)
        for i, p in enumerate(split3(lse_row)):
            stats[h, i:i + 1] = p.astype(jnp.float32)
        for i, p in enumerate(delta_pieces):
            stats[h, 3 + i:4 + i] = p[h:h + 1]
    for load in loads[3:]:
        load.wait()
    for j in range(HEADS):
        h = perm_ref[j]
        c = pl.ds(pl.multiple_of(h * HEAD_DIM, HEAD_DIM), HEAD_DIM)
        g = g_all[:, c]
        own[j, ROW_Q:ROW_Q + TOK] = q_all[:, c]
        own[j, ROW_G:ROW_G + TOK] = g
        kv[j, 0] = jnp.where(keep, k_all[:, c].astype(jnp.float32), 0.0).astype(jnp.bfloat16)
        kv[j, 1] = v_all[:, c]
        own[j, ROW_S:ROW_S + 16] = stats[h].astype(jnp.bfloat16)
        far = jnp.zeros((PEN_ROWS, TOK), jnp.float32)
        for e, ((at, ah), (dt, dh)) in enumerate(PAIRS):
            at, ah = ta + at * s, ha + ah * s
            inside = (at >= 0) & (at < TILES_T) & (ah >= 0) & (ah < TILES_H)
            seen = inside & (reach_ref[0, h] >= abs(dt)) & (reach_ref[1, h] >= abs(dh))
            far = jnp.where(sub_ids == e, jnp.where(seen, jnp.float32(0.0), jnp.float32(FAR)), far)
        pen[j] = far


def restored(slot_ref, counts_ref, res, dq_ref, dk_ref, dv_ref):
    live = counts_ref[lax.axis_index("ta"), lax.axis_index("ha")]
    keep = lax.broadcasted_iota(jnp.int32, (TOK, HEAD_DIM), 0) < live
    for h in range(HEADS):
        j = slot_ref[h]
        c = slice(h * HEAD_DIM, (h + 1) * HEAD_DIM)
        dq_ref[0, 0, :, c] = res[j, 0]
        for i, out in ((1, dk_ref), (2, dv_ref)):
            out[0, 0, :, c] = jnp.where(keep, res[j, i].astype(jnp.float32), 0.0).astype(jnp.bfloat16)


def price(variant):
    A, C = variant
    return 7 * A + 3 * C


VMEM, SMEM = pl.BlockSpec(memory_space=pltpu.VMEM), pl.BlockSpec(memory_space=pltpu.SMEM)
OWN = (HEADS, ROWS, HEAD_DIM)


def exchange(index, own, kv, pen):
    A, C = VARIANTS[index]
    dma, c = pltpu.SemaphoreType.DMA, max(C, 1)

    def terms(*lead):
        return pltpu.VMEM((*lead, TOK, HEAD_DIM), jnp.bfloat16)

    return pl.pallas_call(
        functools.partial(kernel, (A, C)),
        out_shape=jax.ShapeDtypeStruct((HEADS, 3, TOK, HEAD_DIM), jnp.bfloat16),
        in_specs=[VMEM] * 3,
        out_specs=VMEM,
        scratch_shapes=[
            terms(A, 2),
            pltpu.VMEM((A, 5, ROWS, HEAD_DIM), jnp.bfloat16),
            pltpu.VMEM((c, 2, ROWS, HEAD_DIM), jnp.bfloat16),
            terms(A, 5), terms(A, 5), terms(A, 2), terms(A, 2), terms(c, 2), terms(c, 2),
            pltpu.VMEM((HEADS, 5, TOK, HEAD_DIM), jnp.float32),
            dma((A, 11)), dma((A, 11)), dma((c, 4)), dma((c, 4)),
        ],
        compiler_params=pltpu.CompilerParams(
            collective_id=index, has_side_effects=True, vmem_limit_bytes=56 * 2**20
        ),
        name=f"exchange_{A}_{C}",
    )(own, kv, pen)


def per_device(queries, key_tiles, value_tiles, outputs, grads_out, log_sums, tile_counts, head_reach):
    params = pltpu.CompilerParams(vmem_limit_bytes=32 * 2**20)
    choice, slots, own, kv, pen = pl.pallas_call(
        ordered,
        out_shape=(
            jax.ShapeDtypeStruct((1,), jnp.int32),
            jax.ShapeDtypeStruct((HEADS,), jnp.int32),
            jax.ShapeDtypeStruct(OWN, jnp.bfloat16),
            jax.ShapeDtypeStruct((HEADS, 2, TOK, HEAD_DIM), jnp.bfloat16),
            jax.ShapeDtypeStruct((HEADS, PEN_ROWS, TOK), jnp.float32),
        ),
        in_specs=[SMEM] * 2 + [pl.BlockSpec(memory_space=pl.ANY)] * 6,
        out_specs=(SMEM, SMEM, VMEM, VMEM, VMEM),
        scratch_shapes=[pltpu.SMEM((HEADS,), jnp.int32)]
        + [pltpu.VMEM((TOK, HEADS * HEAD_DIM), jnp.bfloat16)] * 5
        + [pltpu.VMEM((HEADS, 1, TOK), jnp.float32), pltpu.VMEM((HEADS, 16, TOK), jnp.float32), pltpu.SemaphoreType.DMA((6,))],
        compiler_params=pltpu.CompilerParams(vmem_limit_bytes=60 * 2**20),
        name="ordered",
    )(
        head_reach.T, tile_counts, queries, key_tiles, value_tiles, outputs, grads_out,
        jnp.transpose(log_sums, (0, 2, 1, 3)).reshape(HEADS, 1, TOK),
    )
    branches = [functools.partial(exchange, i) for i in range(len(VARIANTS))]
    res = branches[0](own, kv, pen) if len(branches) == 1 else lax.switch(choice[0], branches, own, kv, pen)
    tile = jax.ShapeDtypeStruct((1, 1, TOK, HEADS * HEAD_DIM), jnp.bfloat16)
    return pl.pallas_call(
        restored,
        out_shape=(tile, tile, tile),
        in_specs=[SMEM, SMEM, VMEM],
        out_specs=(VMEM, VMEM, VMEM),
        compiler_params=params,
        name="restored",
    )(slots, tile_counts, res)


def solution(mesh):
    tiles = P(("grp", "ta"), "ha", None, None)
    return jax.shard_map(
        per_device, mesh=mesh,
        in_specs=(tiles,) * 6 + (P("grp", None), P()),
        out_specs=(tiles,) * 3, check_vma=False,
    )
```

```python
import functools
import math

import jax
import jax.numpy as jnp
from jax import lax
from jax.experimental import pallas as pl
from jax.experimental.pallas import tpu as pltpu
from jax.sharding import PartitionSpec as P

HEADS = 12
HEAD_DIM = 128
TOK = 128
TILES_T = 4
TILES_H = 8
MESH = pl.DeviceIdType.MESH
FAR = 1e30
LOG2E = math.log2(math.e)
SCALE = HEAD_DIM ** (-0.5)

ROW_Q, ROW_G, ROW_S, ROWS = 0, 128, 256, 272

VARIANTS = (
    (12, 0), (9, 2), (8, 2), (8, 1), (7, 4), (7, 3), (7, 2), (7, 1),
    (6, 4), (6, 3), (6, 2), (5, 4), (5, 3), (5, 2), (4, 4), (4, 2),
)

PAIRS = (
    ((-1, 1), (-1, 1)), ((-1, 0), (-1, 0)), ((-1, -1), (-1, -1)),
    ((0, 0), (0, -1)), ((-1, 1), (-1, 0)), ((-1, 0), (-1, -1)), ((0, 2), (0, 1)), ((-1, 2), (-1, 1)),
    ((0, 1), (0, 1)), ((0, -1), (0, -1)),
)
PEN_ROWS = 16


def nt(a, b):
    return lax.dot_general(a, b, (((1,), (1,)), ((), ())), preferred_element_type=jnp.float32)


def nn(a, b):
    return jnp.dot(a, b, preferred_element_type=jnp.float32)


def tn(a, b):
    return lax.dot_general(a, b, (((0,), (0,)), ((), ())), preferred_element_type=jnp.float32)


def split3(x):
    hi = x.astype(jnp.bfloat16)
    rest = x - hi.astype(jnp.float32)
    mid = rest.astype(jnp.bfloat16)
    lo = (rest - mid.astype(jnp.float32)).astype(jnp.bfloat16)
    return [hi, mid, lo]


def loop(low, high, body):
    if high > low:
        lax.fori_loop(low, high, lambda i, c: (body(i), c)[1], 0)


def kernel(
    counts,
    own, kv, pen, res,
    rkv, rq, rq01, oq, iq, ogr, igr, o01, i01, held,
    ss, rs, ss01, rs01,
):
    A, C = counts
    grp, ta, ha = lax.axis_index("grp"), lax.axis_index("ta"), lax.axis_index("ha")
    x, p = ha // 2, lax.rem(ha, 2)
    z = ta * 2 + p
    s = 1 - 2 * p

    def dev(dx, dz):
        zz = lax.rem(z + dz * s + 8, 8)
        xx = lax.rem(x + dx * s + 4, 4)
        return (grp, zz // 2, xx * 2 + lax.rem(zz, 2))

    zf, zb, xf, xb, z2f, z2b = dev(0, 1), dev(0, -1), dev(1, 0), dev(-1, 0), dev(0, 2), dev(0, -2)

    barrier = pltpu.get_barrier_semaphore()
    for d in (zf, zb, xf, xb, z2f, z2b):
        pl.semaphore_signal(barrier, inc=1, device_id=d, device_id_type=MESH)

    def remote(src, dst, ssem, rsem, to):
        return pltpu.make_async_remote_copy(
            src_ref=src, dst_ref=dst, send_sem=ssem, recv_sem=rsem, device_id=to, device_id_type=MESH
        )

    def copy(i, t):
        src, dst, to = (
            (kv.at[t], rkv.at[t], zf),
            (own.at[t], rq.at[t, 0], zb),
            (own.at[t], rq.at[t, 1], z2f),
            (own.at[t], rq.at[t, 2], xb),
            (rq.at[t, 1], rq.at[t, 3], xb),
            (rq.at[t, 0], rq.at[t, 4], xf),
        )[i]
        return remote(src, dst, ss.at[t, i], rs.at[t, i], to)

    def back(i, t):
        src, dst, to = (
            (oq.at[t, pl.ds(0, 2)], iq.at[t, pl.ds(0, 2)], xf),
            (oq.at[t, 2], iq.at[t, 2], xb),
            (oq.at[t, 3], iq.at[t, 3], zb),
            (oq.at[t, 4], iq.at[t, 4], z2b),
            (ogr.at[t], igr.at[t], zf),
        )[i]
        return remote(src, dst, ss.at[t, 6 + i], rs.at[t, 6 + i], to)

    def copy01(e, t):
        src = own.at[A + t] if e == 0 else rq01.at[t, 0]
        return remote(src, rq01.at[t, e], ss01.at[t, e], rs01.at[t, e], (zf, xf)[e])

    def back01(e, t):
        return remote(o01.at[t, e], i01.at[t, e], ss01.at[t, 2 + e], rs01.at[t, 2 + e], (zf, xb)[e])

    def attend(j, keys, blocks):
        k0, v0 = keys[0], keys[1]
        lse_rows, delta_rows = [], []
        for ref, row in blocks:
            rows = ref[ROW_S:ROW_S + 16].astype(jnp.float32)
            lse_row = rows[0:1] + rows[1:2] + rows[2:3]
            lse_rows.append(lse_row if row is None else lse_row + pen[j, row:row + 1])
            delta_rows.append(rows[3:4] + rows[4:5] + rows[5:6])
        qs = jnp.concatenate([ref[ROW_Q:ROW_Q + TOK] for ref, _ in blocks], axis=0)
        gs = jnp.concatenate([ref[ROW_G:ROW_G + TOK] for ref, _ in blocks], axis=0)
        lse_row, delta_row = jnp.concatenate(lse_rows, axis=1), jnp.concatenate(delta_rows, axis=1)
        prob = jnp.exp2(nt(k0, qs) * (SCALE * LOG2E) - lse_row)
        ds = (prob * (nt(v0, gs) - delta_row) * SCALE).astype(jnp.bfloat16)
        dv = nn(prob.astype(jnp.bfloat16), gs)
        dk = nn(ds, qs)
        dq = tn(ds, k0)
        return dk, dv, [dq[i * TOK:(i + 1) * TOK] for i in range(len(blocks))]

    def bf16(v):
        return v.astype(jnp.bfloat16)

    def f32(v):
        return v.astype(jnp.float32)

    def plain(j):
        dk, dv, dq = attend(j, kv.at[j], [(own.at[j], None)])
        res[j, 0], res[j, 1], res[j, 2] = bf16(dq[0]), bf16(dk), bf16(dv)

    pl.semaphore_wait(barrier, 6)

    def start(t):
        for i in (2, 1, 0, 3):
            copy(i, t).start()

    def relay01(t):
        copy01(0, t).wait_recv()
        copy01(1, t).start()

    def attend01(t):
        copy01(1, t).wait_recv()
        j = A + t
        dk, dv, dq = attend(j, kv.at[j], [(own.at[j], None), (rq01.at[t, 0], 8), (rq01.at[t, 1], 9)])
        res[j, 1], res[j, 2] = bf16(dk), bf16(dv)
        o01[t, 1] = bf16(dq[2])
        back01(1, t).start()
        held[j, 0] = dq[0]
        held[j, 1] = dq[1]

    def merge01(t):
        back01(1, t).wait_recv()
        o01[t, 0] = bf16(held[A + t, 1] + f32(i01[t, 1]))
        back01(0, t).start()

    ahead, out01 = (2, 2) if A > 4 else (min(A, 3), 1)
    loop(0, ahead, start)
    loop(A + C, HEADS, plain)

    def step(t):
        @pl.when(t < A)
        def _():
            copy(2, t).wait_recv()
            copy(4, t).start()
            copy(1, t).wait_recv()
            copy(5, t).start()

        if ahead < A:
            @pl.when(t < A - ahead)
            def _():
                start(t + ahead)

        @pl.when(t == out01)
        def _():
            loop(0, C, lambda i: copy01(0, i).start())

        @pl.when(t == out01 + 1)
        def _():
            loop(0, C, relay01)

        @pl.when((t >= 1) & (t < A + 1))
        def _():
            u = t - 1
            for i in (0, 3, 5, 4):
                copy(i, u).wait_recv()
            tiles = [rq.at[u, i] for i in range(5)]
            dk, dv, dq = attend(
                u, rkv.at[u],
                [(own.at[u], 3), (tiles[0], 4), (tiles[1], 5), (tiles[2], 6), (tiles[3], 7)],
            )
            oq[u, 0] = bf16(dq[3])
            oq[u, 1] = bf16(dq[4])
            back(0, u).start()
            ogr[u, 0] = bf16(dk)
            ogr[u, 1] = bf16(dv)
            back(4, u).start()
            for i in range(3):
                held[u, i] = dq[i]
            dk, dv, dq = attend(
                u, kv.at[u], [(own.at[u], None), (tiles[0], 0), (tiles[1], 1), (tiles[4], 2)]
            )
            oq[u, 2] = bf16(dq[3])
            back(1, u).start()
            for i in range(3):
                held[u, i] = held[u, i] + dq[i]
            held[u, 3] = dk
            held[u, 4] = dv

        @pl.when(t == out01 + 2)
        def _():
            loop(0, C, attend01)

        @pl.when((t >= 2) & (t < A + 2))
        def _():
            u = t - 2
            back(0, u).wait_recv()
            oq[u, 4] = bf16(held[u, 2] + f32(iq[u, 1]))
            back(3, u).start()
            back(1, u).wait_recv()
            oq[u, 3] = bf16(held[u, 1] + f32(iq[u, 2]))
            back(2, u).start()

        @pl.when(t == out01 + 3)
        def _():
            loop(0, C, merge01)

        @pl.when(t >= 3)
        def _():
            u = t - 3
            back(4, u).wait_recv()
            res[u, 1] = bf16(held[u, 3] + f32(igr[u, 0]))
            res[u, 2] = bf16(held[u, 4] + f32(igr[u, 1]))
            back(2, u).wait_recv()
            back(3, u).wait_recv()
            res[u, 0] = bf16(held[u, 0] + f32(iq[u, 0]) + f32(iq[u, 3]) + f32(iq[u, 4]))

    loop(0, A + 3, step)

    def finish01(t):
        back01(0, t).wait_recv()
        res[A + t, 0] = bf16(held[A + t, 0] + f32(i01[t, 0]))

    loop(0, C, finish01)

    def drain(t):
        for i in range(6):
            copy(i, t).wait_send()
        for i in range(5):
            back(i, t).wait_send()

    def drain01(t):
        for e in range(2):
            copy01(e, t).wait_send()
            back01(e, t).wait_send()

    loop(0, A, drain)
    loop(0, C, drain01)


def ordered(
    reach_any, counts_any, q_ref, k_ref, v_ref, o_ref, g_ref, lse_ref,
    choice_ref, slot_ref, own, kv, pen,
    perm_ref, reach_ref, counts_ref, q_all, k_all, v_all, o_all, g_all, lse_all, stats, sems,
):
    loads = [
        pltpu.make_async_copy(src, dst, sems.at[i])
        for i, (src, dst) in enumerate((
            (lse_ref, lse_all), (g_ref.at[0, 0], g_all), (o_ref.at[0, 0], o_all),
            (q_ref.at[0, 0], q_all), (k_ref.at[0, 0], k_all), (v_ref.at[0, 0], v_all),
        ))
    ]
    scalars = [
        pltpu.make_async_copy(reach_any, reach_ref, sems.at[6]),
        pltpu.make_async_copy(counts_any, counts_ref, sems.at[7]),
    ]
    for load in scalars + loads:
        load.start()
    for load in scalars:
        load.wait()
    ta, ha = lax.axis_index("ta"), lax.axis_index("ha")
    s = 1 - 2 * lax.rem(ha, 2)
    live = counts_ref[ta, ha]
    rt = [reach_ref[0, h] for h in range(HEADS)]
    rh = [reach_ref[1, h] for h in range(HEADS)]
    n1 = sum(rt)
    n01 = sum(rh) - sum(t * h for t, h in zip(rt, rh))
    choice, A, C = [jnp.int32(v) for v in (0, *VARIANTS[0])]
    for i in sorted(range(len(VARIANTS)), key=lambda i: -price(VARIANTS[i])):
        a, c = VARIANTS[i]
        fits = n1 + jnp.maximum(n01 - c, 0) <= a
        choice, A, C = [jnp.where(fits, new, old) for new, old in zip((i, a, c), (choice, A, C))]
    choice_ref[0] = choice
    c1, c01, c00 = [jnp.int32(0)] * 3
    first = []
    for h in range(HEADS):
        own01 = (rt[h] == 0) & (rh[h] == 1) & (c01 < C)
        none = (rt[h] == 0) & (rh[h] == 0)
        first.append(jnp.where(none, -1, jnp.where(own01, A + c01, c1)))
        c01 = c01 + jnp.where(own01, 1, 0)
        c1 = c1 + jnp.where(own01 | none, 0, 1)
    for h in range(HEADS):
        none = first[h] < 0
        in1 = none & (c1 < A)
        in01 = none & (c1 >= A) & (c01 < C)
        in00 = none & (c1 >= A) & (c01 >= C)
        slot = jnp.where(none, jnp.where(in1, c1, jnp.where(in01, A + c01, A + C + c00)), first[h])
        c1, c01, c00 = [n + jnp.where(taken, 1, 0) for n, taken in ((c1, in1), (c01, in01), (c00, in00))]
        slot_ref[h] = slot
        perm_ref[slot] = h
    keep = lax.broadcasted_iota(jnp.int32, (TOK, HEAD_DIM), 0) < live
    lane_ids = lax.broadcasted_iota(jnp.int32, (1, TOK), 1)
    sub_ids = lax.broadcasted_iota(jnp.int32, (PEN_ROWS, TOK), 0)
    for load in loads[:3]:
        load.wait()
    feature = lax.broadcasted_iota(jnp.int32, (16, HEADS * HEAD_DIM), 1) // HEAD_DIM
    member = jnp.where(feature == lax.broadcasted_iota(jnp.int32, (16, HEADS * HEAD_DIM), 0), 1.0, 0.0)
    member = member.astype(jnp.bfloat16)
    prod = g_all[...].astype(jnp.float32) * o_all[...].astype(jnp.float32)
    high = prod.astype(jnp.bfloat16)
    low = (prod - high.astype(jnp.float32)).astype(jnp.bfloat16)
    delta = nt(member, high) + nt(member, low)
    delta_pieces = [p.astype(jnp.float32) for p in split3(delta)]
    stats[...] = jnp.zeros_like(stats)
    for h in range(HEADS):
        lse_row = jnp.where(lane_ids < live, lse_all[h] * LOG2E, FAR)
        for i, p in enumerate(split3(lse_row)):
            stats[h, i:i + 1] = p.astype(jnp.float32)
        for i, p in enumerate(delta_pieces):
            stats[h, 3 + i:4 + i] = p[h:h + 1]
    for load in loads[3:]:
        load.wait()
    at, ah, step_t, step_h = [jnp.zeros((PEN_ROWS, TOK), jnp.int32)] * 4
    for e, ((place_t, place_h), (dt, dh)) in enumerate(PAIRS):
        row = sub_ids == e
        at, ah = jnp.where(row, ta + place_t * s, at), jnp.where(row, ha + place_h * s, ah)
        step_t, step_h = jnp.where(row, abs(dt), step_t), jnp.where(row, abs(dh), step_h)
    inside = (at >= 0) & (at < TILES_T) & (ah >= 0) & (ah < TILES_H)
    for j in range(HEADS):
        h = perm_ref[j]
        c = pl.ds(pl.multiple_of(h * HEAD_DIM, HEAD_DIM), HEAD_DIM)
        g = g_all[:, c]
        own[j, ROW_Q:ROW_Q + TOK] = q_all[:, c]
        own[j, ROW_G:ROW_G + TOK] = g
        kv[j, 0] = jnp.where(keep, k_all[:, c].astype(jnp.float32), 0.0).astype(jnp.bfloat16)
        kv[j, 1] = v_all[:, c]
        own[j, ROW_S:ROW_S + 16] = stats[h].astype(jnp.bfloat16)
        seen = inside & ((step_t == 0) | (reach_ref[0, h] == 1)) & ((step_h == 0) | (reach_ref[1, h] == 1))
        far = jnp.where(seen, 0.0, jnp.float32(FAR))
        pen[j] = far


def restored(slot_ref, counts_ref, res, dq_ref, dk_ref, dv_ref):
    live = counts_ref[lax.axis_index("ta"), lax.axis_index("ha")]
    keep = lax.broadcasted_iota(jnp.int32, (TOK, HEAD_DIM), 0) < live
    for h in range(HEADS):
        j = slot_ref[h]
        c = slice(h * HEAD_DIM, (h + 1) * HEAD_DIM)
        dq_ref[0, 0, :, c] = res[j, 0]
        for i, out in ((1, dk_ref), (2, dv_ref)):
            out[0, 0, :, c] = jnp.where(keep, res[j, i].astype(jnp.float32), 0.0).astype(jnp.bfloat16)


def price(variant):
    A, C = variant
    return 7 * A + 3 * C


VMEM, SMEM = pl.BlockSpec(memory_space=pltpu.VMEM), pl.BlockSpec(memory_space=pltpu.SMEM)
OWN = (HEADS, ROWS, HEAD_DIM)


def exchange(index, own, kv, pen):
    A, C = VARIANTS[index]
    dma, c = pltpu.SemaphoreType.DMA, max(C, 1)

    def terms(*lead):
        return pltpu.VMEM((*lead, TOK, HEAD_DIM), jnp.bfloat16)

    return pl.pallas_call(
        functools.partial(kernel, (A, C)),
        out_shape=jax.ShapeDtypeStruct((HEADS, 3, TOK, HEAD_DIM), jnp.bfloat16),
        in_specs=[VMEM] * 3,
        out_specs=VMEM,
        scratch_shapes=[
            terms(A, 2),
            pltpu.VMEM((A, 5, ROWS, HEAD_DIM), jnp.bfloat16),
            pltpu.VMEM((c, 2, ROWS, HEAD_DIM), jnp.bfloat16),
            terms(A, 5), terms(A, 5), terms(A, 2), terms(A, 2), terms(c, 2), terms(c, 2),
            pltpu.VMEM((HEADS, 5, TOK, HEAD_DIM), jnp.float32),
            dma((A, 11)), dma((A, 11)), dma((c, 4)), dma((c, 4)),
        ],
        compiler_params=pltpu.CompilerParams(
            collective_id=index, has_side_effects=True, vmem_limit_bytes=56 * 2**20
        ),
        name=f"exchange_{A}_{C}",
    )(own, kv, pen)


def per_device(queries, key_tiles, value_tiles, outputs, grads_out, log_sums, tile_counts, head_reach):
    params = pltpu.CompilerParams(vmem_limit_bytes=32 * 2**20)
    choice, slots, own, kv, pen = pl.pallas_call(
        ordered,
        out_shape=(
            jax.ShapeDtypeStruct((1,), jnp.int32),
            jax.ShapeDtypeStruct((HEADS,), jnp.int32),
            jax.ShapeDtypeStruct(OWN, jnp.bfloat16),
            jax.ShapeDtypeStruct((HEADS, 2, TOK, HEAD_DIM), jnp.bfloat16),
            jax.ShapeDtypeStruct((HEADS, PEN_ROWS, TOK), jnp.float32),
        ),
        in_specs=[pl.BlockSpec(memory_space=pl.ANY)] * 8,
        out_specs=(SMEM, SMEM, VMEM, VMEM, VMEM),
        scratch_shapes=[
            pltpu.SMEM((HEADS,), jnp.int32), pltpu.SMEM((2, HEADS), jnp.int32), pltpu.SMEM((TILES_T, TILES_H), jnp.int32)
        ]
        + [pltpu.VMEM((TOK, HEADS * HEAD_DIM), jnp.bfloat16)] * 5
        + [pltpu.VMEM((HEADS, 1, TOK), jnp.float32), pltpu.VMEM((HEADS, 16, TOK), jnp.float32), pltpu.SemaphoreType.DMA((8,))],
        compiler_params=pltpu.CompilerParams(vmem_limit_bytes=60 * 2**20),
        name="ordered",
    )(
        head_reach.T, tile_counts, queries, key_tiles, value_tiles, outputs, grads_out,
        jnp.transpose(log_sums, (0, 2, 1, 3)).reshape(HEADS, 1, TOK),
    )
    branches = [functools.partial(exchange, i) for i in range(len(VARIANTS))]
    res = branches[0](own, kv, pen) if len(branches) == 1 else lax.switch(choice[0], branches, own, kv, pen)
    tile = jax.ShapeDtypeStruct((1, 1, TOK, HEADS * HEAD_DIM), jnp.bfloat16)
    return pl.pallas_call(
        restored,
        out_shape=(tile, tile, tile),
        in_specs=[SMEM, SMEM, VMEM],
        out_specs=(VMEM, VMEM, VMEM),
        compiler_params=params,
        name="restored",
    )(slots, tile_counts, res)


def solution(mesh):
    tiles = P(("grp", "ta"), "ha", None, None)
    return jax.shard_map(
        per_device, mesh=mesh,
        in_specs=(tiles,) * 6 + (P("grp", None), P()),
        out_specs=(tiles,) * 3, check_vma=False,
    )
```
